32 devices in a mesh: groups: 2 (over y), wide: 4 (over z), narrow: 2 (over x), lev: 2 (over core).
Axes of the slice: x: 2, y: 2, z: 4, core: 2. Of those that a mesh axis runs over, the one named last changes fastest.
Arguments:
- parent_state: float32 [2, 64, 128, 256], P(None, 'lev', ('groups', 'wide'), 'narrow'), parts along dimension 2, may hold values from -6 to 6
- nest_state: float32 [2, 64, 64, 512], P(None, 'lev', ('groups', 'wide'), 'narrow'), parts along dimension 2, may hold values from -6 to 6
- level_weights: float32 [64], P('lev'), may hold values from -0.75 to 0.75
- diffusion: float32 [64], P('lev'), may hold values from 0.02 to 0.06
- smoothing: float32 [64], P('lev'), may hold values from 0.0008 to 0.0024
- coupling: float32 [64], P('lev'), may hold values from 0.02 to 0.06
- transport: float32 [64], P('lev'), may hold values from 0.1 to 0.3
- nest_anchor: int32 [2], P('groups'), parts along dimension 0, may hold values from 1 to 47
Outputs:
- parent_out: float32 [2, 64, 128, 256], P(None, 'lev', ('groups', 'wide'), 'narrow'), parts along dimension 2
- nest_out: float32 [2, 64, 64, 512], P(None, 'lev', ('groups', 'wide'), 'narrow'), parts along dimension 2
The draws below stay inside these ranges and needn't reach their ends.
There are 2 independent parts, one for each index of `groups`. The reference program is written for one: setup_inputs(seed, part) draws one part's arguments, and reference() takes and returns one part's arrays. A program takes and returns all parts, laid end to end along the dimension named above; an argument that names none is the same for every part. Nothing has to cross between parts.
Inputs may be any that keep to these rules, and one draw needn't show every extreme that they name: `nest_anchor`: the rows just outside the nest on both sides lie inside the parent grid.
All inputs are finite; a program needn't handle non-finite values.
Results may differ from the reference program's by a relative error of at most 0.00002.
Values sent between devices are 32-bit elements; how exact they have to be, the bound alone decides.
A program may use at most 64 MiB of HBM per device.

```python
import math
import jax
import jax.numpy as jnp
from jax import lax

LEV = 64
NR = 64
NC = 256
NEST_ROWS = 32
NEST_COLS = 512
BAND = 16


def steps_of(stream_key, extent, split, low, high):
    def one(dim, parts):
        draws = jax.random.uniform(jax.random.fold_in(jax.random.fold_in(stream_key, 6), dim), (parts,), jnp.float32, low / len(split), high / len(split))
        return jnp.repeat(jnp.exp(draws), extent[dim] // parts).reshape((-1,) + (1,) * (len(extent) - dim - 1))

    level = one(*split[0])
    for cut in split[1:]:
        level = level * one(*cut)
    return level


def scatter_about(stream_key, dims, width, reach, pieces=(), dtype=jnp.bfloat16):
    array = width * jax.random.normal(stream_key, dims, jnp.float32)
    if pieces:
        array = array * steps_of(stream_key, dims, pieces, -0.22, 0.18)
    return jnp.clip(array, -reach, reach).astype(dtype)


def setup_inputs(seed: int = 0, part: int = 0) -> dict:
    arg_keys = jax.random.split(jax.random.key(seed), 9)
    part_splits = jax.random.split(jax.random.fold_in(arg_keys[8], part), 9)
    parent_state = scatter_about(part_splits[0], (2, LEV, NR, NC), 1.0, 6.0, ((1, 2), (2, 4), (3, 2)), jnp.float32)
    nest_state = scatter_about(part_splits[1], (2, LEV, NEST_ROWS, NEST_COLS), 1.0, 6.0, ((1, 2), (2, 4), (3, 2)), jnp.float32)
    level_weights = scatter_about(arg_keys[2], (LEV,), LEV ** -0.5, 0.75, ((0, 2),), jnp.float32)
    diffusion = jnp.clip(jnp.exp(math.log(0.06) - 1.0986123 * jax.random.uniform(arg_keys[3], (LEV,), jnp.float32) ** steps_of(arg_keys[3], (LEV,), ((0, 2),), -0.2, 0.2)), 0.02, 0.06)
    smoothing = jnp.clip(jnp.exp(math.log(0.0024) - 1.09861236 * jax.random.uniform(arg_keys[4], (LEV,), jnp.float32) ** steps_of(arg_keys[4], (LEV,), ((0, 2),), -0.2, 0.2)), 0.0008, 0.0024)
    coupling = jnp.clip(jnp.exp(math.log(0.06) - 1.0986123 * jax.random.uniform(arg_keys[5], (LEV,), jnp.float32) ** steps_of(arg_keys[5], (LEV,), ((0, 2),), -0.2, 0.2)), 0.02, 0.06)
    transport = jnp.clip(jnp.exp(math.log(0.3) - 1.0986123 * jax.random.uniform(arg_keys[6], (LEV,), jnp.float32) ** steps_of(arg_keys[6], (LEV,), ((0, 2),), -0.2, 0.2)), 0.1, 0.3)
    nest_anchor = jax.random.randint(part_splits[7], (1,), 1, NR - BAND).astype(jnp.int32)
    return {"parent_state": parent_state, "nest_state": nest_state, "level_weights": level_weights, "diffusion": diffusion, "smoothing": smoothing, "coupling": coupling, "transport": transport, "nest_anchor": nest_anchor}


def laplace(values):
    return (values[..., 2:, 1:-1] + values[..., :-2, 1:-1] + values[..., 1:-1, 2:]
            + values[..., 1:-1, :-2] - 4.0 * values[..., 1:-1, 1:-1])


def central(values, direction):
    if direction == 0:
        return 0.5 * (values[..., 3:-1, 2:-2] - values[..., 1:-3, 2:-2])
    return 0.5 * (values[..., 2:-2, 3:-1] - values[..., 2:-2, 1:-3])


def column_part(extended, level_weights):
    return jnp.sum(level_weights[:, None, None] * extended[0], axis=0)


def advance(extended, column, coefficients):
    diffuse = coefficients[0][:, None, None]
    smooth = coefficients[1][:, None, None]
    couple = coefficients[2][:, None, None]
    advect = coefficients[3][:, None, None]
    height = extended[0]
    tracer = extended[1]
    lap_height = laplace(height)
    new_height = (height[:, 2:-2, 2:-2] + diffuse * lap_height[:, 1:-1, 1:-1]
                  - smooth * laplace(lap_height) + couple * laplace(column)[1:-1, 1:-1])
    drift_term = central(column, 0) * central(tracer, 0) + central(column, 1) * central(tracer, 1)
    new_tracer = tracer[:, 2:-2, 2:-2] + diffuse * laplace(tracer)[:, 1:-1, 1:-1] - advect * drift_term
    return jnp.stack([new_height, new_tracer])


def extend(state, top_row, bottom_row):
    stacked = jnp.concatenate([top_row[:, :, None], top_row[:, :, None], state,
                               bottom_row[:, :, None], bottom_row[:, :, None]], axis=2)
    return jnp.concatenate([stacked[..., -2:], stacked, stacked[..., :2]], axis=3)


def widen_row(values):
    return jnp.repeat(values, 2, axis=-1)


def reference(parent_state, nest_state, level_weights, diffusion, smoothing, coupling, transport, nest_anchor):
    anchor = nest_anchor[0].astype(jnp.int32)
    band_rows = nest_state.shape[2] // 2
    coarse_coefficients = (diffusion, smoothing, coupling, transport)
    fine_coefficients = (2.0 * diffusion, 8.0 * smoothing, 2.0 * coupling, 2.0 * transport)
    zero_row = jnp.zeros((parent_state.shape[0], parent_state.shape[1], parent_state.shape[3]), jnp.float32)
    parent_ext = extend(parent_state, zero_row, zero_row)
    parent_new = advance(parent_ext, column_part(parent_ext, level_weights), coarse_coefficients)
    north_old = lax.dynamic_index_in_dim(parent_state, anchor - 1, 2, keepdims=False)
    south_old = lax.dynamic_index_in_dim(parent_state, anchor + band_rows, 2, keepdims=False)
    north_new = lax.dynamic_index_in_dim(parent_new, anchor - 1, 2, keepdims=False)
    south_new = lax.dynamic_index_in_dim(parent_new, anchor + band_rows, 2, keepdims=False)
    nest_ext = extend(nest_state, widen_row(north_old), widen_row(south_old))
    nest_mid = advance(nest_ext, column_part(nest_ext, level_weights), fine_coefficients)
    nest_ext = extend(nest_mid, widen_row(0.5 * (north_old + north_new)), widen_row(0.5 * (south_old + south_new)))
    nest_out = advance(nest_ext, column_part(nest_ext, level_weights), fine_coefficients)
    coarse = 0.25 * (nest_out[:, :, 0::2, 0::2] + nest_out[:, :, 1::2, 0::2]
                     + nest_out[:, :, 0::2, 1::2] + nest_out[:, :, 1::2, 1::2])
    parent_out = lax.dynamic_update_slice_in_dim(parent_new, coarse, anchor, 2)
    return parent_out, nest_out
```

```python
import functools
import jax
import jax.numpy as jnp
from jax import lax
from jax.experimental import pallas as pl
from jax.experimental.pallas import tpu as pltpu
from jax.sharding import PartitionSpec as P

T = 128


def roll(x, shift):
    return pltpu.roll(x, shift, axis=1)


def kernel(
    W, N, anchor_ref, cf_ref, p_ref, n_ref, po_ref, no_ref,
    pe, ne, ne2, lp, ln, cb, pack, pack2, cr, cr2,
    psp, prp, psn, prn, psm, prm, pick, tips, slots0, slots1, corners0, corners1, cg, ssem, rsem,
):
    R, K, C = p_ref.shape[1:]
    r, c = n_ref.shape[1], n_ref.shape[3]
    half = r // 2
    slots, corners = (slots0, slots1), (corners0, corners1)
    band = half * W
    w, n, lev = lax.axis_index("wide"), lax.axis_index("narrow"), lax.axis_index("lev")
    anchor = anchor_ref[0]
    steps = (1,) if N == 2 else (1, N - 1)
    other = {"lev": 1 - lev}
    lane = lax.broadcasted_iota(jnp.int32, (K, T), 1)

    barrier = pltpu.get_barrier_semaphore()
    count = 0
    for dw in range(W):
        for dn in (0,) + steps:
            if dw or dn:
                pl.semaphore_signal(
                    barrier, inc=1, device_id_type=pl.DeviceIdType.MESH,
                    device_id={"wide": lax.rem(w + dw, W), "narrow": lax.rem(n + dn, N)},
                )
                count += 1
    pl.semaphore_signal(barrier, inc=1, device_id=other, device_id_type=pl.DeviceIdType.MESH)

    next_send, next_recv, pending = [0], [0], []

    def take(many=1):
        next_recv[0] += many
        return next_recv[0] - many

    def guarded(cond, act):
        if cond is None:
            act()
        else:
            pl.when(cond)(act)

    def send(src, dst, sem, device, cond=None):
        copy = pltpu.make_async_remote_copy(
            src_ref=src, dst_ref=dst, send_sem=ssem.at[next_send[0]], recv_sem=rsem.at[sem],
            device_id=device, device_id_type=pl.DeviceIdType.MESH,
        )
        next_send[0] += 1
        guarded(cond, lambda: copy.start())
        pending.append((copy, cond))

    def receive(dst, sem, cond=None):
        copy = pltpu.make_async_remote_copy(
            src_ref=dst, dst_ref=dst, send_sem=ssem.at[0], recv_sem=rsem.at[sem],
            device_id=other, device_id_type=pl.DeviceIdType.MESH,
        )
        guarded(cond, lambda: copy.wait_recv())

    above, below = w > 0, w < W - 1
    up, down = {"wide": w - 1}, {"wide": w + 1}
    waits = []

    def send_rows(src, start, dst, rows, lanes):
        s = take(4)
        at = lambda ref, f, i, m: ref.at[f, pl.ds(i, m), :, pl.ds(0, lanes)]
        for f, m, k in ((0, 2, 0), (1, 1, 1)):
            send(at(src, f, start + rows - m, m), at(dst, f, 2 - m, m), s + k, down, below)
            send(at(src, f, start, m), at(dst, f, rows + 2, m), s + 2 + k, up, above)

        def wait():
            for f, m, k in ((0, 2, 0), (1, 1, 1)):
                receive(at(dst, f, 2 - m, m), s + k, above)
                receive(at(dst, f, rows + 2, m), s + 2 + k, below)
        return wait

    def send_packs(src, dst, first):
        todo = []
        for d, dn in enumerate(steps):
            to = lax.rem(n + dn, N)
            s = take(3)
            send(src, dst.at[d, 1], s + 1, {"narrow": to})
            tip = src.at[pl.ds(first, 1)]
            send(tip, dst.at[d, 0, pl.ds(first, 1)], s, {"wide": w + 1, "narrow": to}, below)
            send(tip, dst.at[d, 2, pl.ds(first, 1)], s + 2, {"wide": w - 1, "narrow": to}, above)
            todo.append((dst.at[d, 1], s + 1, None))
            todo.append((dst.at[d, 0, pl.ds(first, 1)], s, above))
            todo.append((dst.at[d, 2, pl.ds(first, 1)], s + 2, below))
        return lambda: [receive(*one) for one in todo]

    def merged(dst, at, tile, even):
        if N == 2:
            return dst[0, at, tile]
        return jnp.where(even, dst[0, at, tile], dst[1, at, tile])

    def ends(value, lanes):
        return jnp.where(lane < T // 2, value[:, :T], value[:, lanes - T:lanes])

    def send_picks(source, k):
        s = take(W)
        sems = [take(W) for _ in steps]
        for e, (row, target, cond) in enumerate((
            (anchor - 1, 0, w != 0), (anchor + band, W - 1, w != W - 1),
        )):
            local = jnp.clip(row - w * R, 0, R - 1)
            for f in range(2):
                pick[k, e, f] = source[f, local]
            tips[k, e] = ends(pick[k, e, 0], C)
            send(pick.at[k, e], slots[k].at[w], s + w, {"wide": target}, cond)
            for d, dn in enumerate(steps):
                send(
                    tips.at[k, e], corners[k].at[d, w], sems[d] + w,
                    {"wide": target, "narrow": lax.rem(n + dn, N)}, cond,
                )
        for e, target in ((0, 0), (1, W - 1)):
            for d, dn in enumerate(steps):
                send(
                    tips.at[k, e], corners[k].at[d, w], sems[d] + w,
                    {"narrow": lax.rem(n + dn, N)}, w == target,
                )

            def keep(e=e):
                slots[k][w] = pick[k, e]
            pl.when(w == target)(keep)

        def wait():
            for target in (0, W - 1):
                for src in range(W):
                    if src != target:
                        receive(slots[k].at[src], s + src, w == target)
                    for d in range(len(steps)):
                        receive(corners[k].at[d, src], sems[d] + src, w == target)
        return wait

    def set_edges(dst, ks):
        scale = 1.0 / len(ks)
        wider = (
            lax.broadcasted_iota(jnp.int32, (C, c), 1) // 2
            == lax.broadcasted_iota(jnp.int32, (C, c), 0)
        ).astype(jnp.float32)
        for row, target, first, near in (
            (anchor - 1, 0, 0, 1), (anchor + band, W - 1, r + 2, r + 2),
        ):
            owner = lax.div(row, R)

            def fill(owner=owner, first=first, near=near):
                for f in range(2):
                    value = scale * sum(slots[k][owner, f] for k in ks)
                    fine = jnp.dot(
                        value, wider, precision=lax.Precision.HIGHEST,
                        preferred_element_type=jnp.float32,
                    )
                    dst[f, first, :, 0:c] = fine
                    dst[f, first + 1, :, 0:c] = fine
                left = scale * sum(corners[k][0, owner] for k in ks)
                if N > 2:
                    right = scale * sum(corners[k][1, owner] for k in ks)
                    left = jnp.where(lane < T // 2, right, left)
                dst[0, near, :, c:c + T] = left
            pl.when(w == target)(fill)

    def column_sums(ext, rows, out):
        weights = cb[0, :, 0:ext.shape[3]]

        def body(j, _):
            out[pl.ds(j, 1), :] = jnp.sum(weights * ext[0, j + 1], axis=0, keepdims=True)
            return 0
        lax.fori_loop(0, rows + 2, body, 0)

    def advance(ext, rows, lanes, mine, theirs, lap, f, g, store):
        L = lanes + T
        near = lambda x: roll(x, 1) + roll(x, L - 1)

        def inner(j, _):
            x = ext[0, j + 1]
            lap[j] = ext[0, j + 2] + ext[0, j] + near(x) - 4.0 * x
            return 0
        lax.fori_loop(0, rows + 2, inner, 0)
        diffuse, smooth = f * cb[1, :, 0:lanes], g * cb[2, :, 0:lanes]
        couple, advect = f * cb[3, :, 0:lanes], f * cb[4, :, 0:lanes]

        def body(i, _):
            total = lambda j: mine[pl.ds(j, 1), :] + theirs[pl.ds(j, 1), :]
            p0, p1, p2 = total(i), total(i + 1), total(i + 2)
            wide1 = jnp.broadcast_to(p1, (8, L))
            pl_, pr = roll(wide1, 1)[0:1, :lanes], roll(wide1, L - 1)[0:1, :lanes]
            p0, p1, p2 = p0[:, :lanes], p1[:, :lanes], p2[:, :lanes]
            lap_p = p2 + p0 + pr + pl_ - 4.0 * p1
            drp, dcp = 0.5 * (p2 - p0), 0.5 * (pr - pl_)
            l1 = lap[i + 1]
            m1 = l1[:, :lanes]
            lap2 = lap[i + 2][:, :lanes] + lap[i][:, :lanes] + near(l1)[:, :lanes] - 4.0 * m1
            h = ext[0, i + 2][:, :lanes]
            store(0, i, h + diffuse * m1 - smooth * lap2 + couple * lap_p)
            q = ext[1, i + 2]
            qu, qd, q1 = ext[1, i + 1][:, :lanes], ext[1, i + 3][:, :lanes], q[:, :lanes]
            ql, qr = roll(q, 1)[:, :lanes], roll(q, L - 1)[:, :lanes]
            lap_q = qd + qu + qr + ql - 4.0 * q1
            drift = drp * (0.5 * (qd - qu)) + dcp * (0.5 * (qr - ql))
            store(1, i, q1 + diffuse * lap_q - advect * drift)
            return 0
        lax.fori_loop(0, rows, body, 0)

    def pack_nest(ref, start, dst, tile):
        dst[tile] = jnp.zeros((K, T), jnp.float32)

        def body(i, _):
            for f in range(2):
                slot = f * r + i
                x = ends(ref[f, i + start], c)
                dst[tile] = jnp.where(lane // 4 == slot, roll(x, 4 * slot + 2), dst[tile])
            return 0
        lax.fori_loop(0, r, body, 0)

    pl.semaphore_wait(barrier, count + 1)
    wait_rows = [send_rows(p_ref, 0, pe, R, C), send_rows(n_ref, 0, ne, r, c)]
    wait_old = send_picks(p_ref, 0)
    pack[0] = jnp.zeros((K, T), jnp.float32)

    def pack_parent(i, _):
        for f in range(2):
            slot = f * R + i
            x = ends(p_ref[f, i], C)
            pack[0] = jnp.where(lane // 4 == slot, roll(x, 4 * slot + 2), pack[0])
        return 0
    lax.fori_loop(0, R, pack_parent, 0)
    pack_nest(n_ref, 0, pack, 1)
    for slot, row in ((2 * r, 0), (2 * r + 1, R - 1)):
        x = ends(p_ref[0, row], C)
        pack[1] = jnp.where(lane // 4 == slot, roll(x, 4 * slot + 2), pack[1])
    wait_packs = send_packs(pack, cr, 1)

    for j in range(5):
        cb[j] = jnp.broadcast_to(cf_ref[:, j:j + 1], cb.shape[1:])
    for f in range(2):
        pe[f, 2:R + 2, :, 0:C] = p_ref[f]
        ne[f, 2:r + 2, :, 0:c] = n_ref[f]
    for cond, first in ((w == 0, 0), (w == W - 1, R + 2)):
        def clear(first=first):
            pe[:, first:first + 2] = jnp.zeros((2, 2, K, C + T), jnp.float32)
        pl.when(cond)(clear)
    left_part = lane % 4 < 2
    side = lambda slot: lax.rem(2 * T - 2 - 4 * slot, T)
    wait_packs()
    m0 = merged(cr, 1, 0, left_part)
    m1 = merged(cr, 1, 1, left_part)

    def unpack_parent(i, _):
        for f in range(2):
            pe[f, i + 2, :, C:C + T] = roll(m0, side(f * R + i))
        return 0
    lax.fori_loop(0, R, unpack_parent, 0)

    def unpack_nest(dst, m):
        def body(i, _):
            for f in range(2):
                dst[f, i + 2, :, c:c + T] = roll(m, side(f * r + i))
            return 0
        lax.fori_loop(0, r, body, 0)
    unpack_nest(ne, m1)

    @pl.when(above)
    def _():
        m = merged(cr, 0, 1, left_part)
        pe[0, 1, :, C:C + T] = roll(m, side(2 * r + 1))
        ne[0, 1, :, c:c + T] = roll(m, side(r - 1))

    @pl.when(below)
    def _():
        m = merged(cr, 2, 1, left_part)
        pe[0, R + 2, :, C:C + T] = roll(m, side(2 * r))
        ne[0, r + 2, :, c:c + T] = roll(m, side(0))

    def share(mine, theirs):
        s = take()
        send(mine, theirs, s, other)
        return lambda: receive(theirs, s)

    wait_rows[0]()
    column_sums(pe, R, psp)
    wait_p = share(psp, prp)
    wait_rows[1]()
    wait_old()
    set_edges(ne, (0,))
    column_sums(ne, r, psn)
    wait_n = share(psn, prn)
    wait_p()

    def store_parent(f, i, v):
        po_ref[f, i] = v

    def store_mid(f, i, v):
        ne2[f, i + 2, :, 0:c] = v

    def store_nest(f, i, v):
        no_ref[f, i] = v

    advance(pe, R, C, psp, prp, lp, 1.0, 1.0, store_parent)
    wait_new = send_picks(po_ref, 1)
    wait_n()
    advance(ne, r, c, psn, prn, ln, 2.0, 8.0, store_mid)
    wait_mid = send_rows(ne2, 2, ne2, r, c)
    pack_nest(ne2, 2, pack2, 0)
    wait_packs2 = send_packs(pack2, cr2, 0)
    wait_new()
    set_edges(ne2, (0, 1))
    wait_packs2()
    unpack_nest(ne2, merged(cr2, 1, 0, left_part))

    @pl.when(above)
    def _():
        ne2[0, 1, :, c:c + T] = roll(merged(cr2, 0, 0, left_part), side(r - 1))

    @pl.when(below)
    def _():
        ne2[0, r + 2, :, c:c + T] = roll(merged(cr2, 2, 0, left_part), side(0))

    wait_mid()
    column_sums(ne2, r, psm)
    wait_m = share(psm, prm)
    wait_m()
    advance(ne2, r, c, psm, prm, ln, 2.0, 8.0, store_nest)
    narrower = jnp.where(
        lax.broadcasted_iota(jnp.int32, (c, C), 0) // 2
        == lax.broadcasted_iota(jnp.int32, (c, C), 1), 0.25, 0.0
    )
    base = w * half
    for i in range(half):
        for f in range(2):
            cg[base + i, f] = jnp.dot(
                no_ref[f, 2 * i] + no_ref[f, 2 * i + 1], narrower,
                precision=lax.Precision.HIGHEST, preferred_element_type=jnp.float32,
            )
    s = take(W)
    for dw in range(1, W):
        block = cg.at[pl.ds(base, half)]
        send(block, block, s + w, {"wide": lax.rem(w + dw, W)})
    for dw in range(1, W):
        src = lax.rem(w + dw, W)
        receive(cg.at[pl.ds(src * half, half)], s + src)

    def absorb(i, _):
        at = w * R + i - anchor
        inside = (at >= 0) & (at < band)
        piece = jnp.clip(at, 0, band - 1)
        for f in range(2):
            po_ref[f, i] = jnp.where(inside, cg[piece, f], po_ref[f, i])
        return 0
    lax.fori_loop(0, R, absorb, 0)
    for copy, cond in pending:
        guarded(cond, lambda copy=copy: copy.wait_send())


def shards(
    W, N, parent_state, nest_state, level_weights, diffusion, smoothing, coupling, transport, nest_anchor
):
    p = jnp.swapaxes(parent_state, 1, 2)
    q = jnp.swapaxes(nest_state, 1, 2)
    cf = jnp.stack([level_weights, diffusion, smoothing, coupling, transport], axis=1)
    _, R, K, C = p.shape
    r, c = q.shape[1], q.shape[3]
    D = 1 if N == 2 else 2
    F = lambda *dims: pltpu.VMEM(dims, jnp.float32)
    up8 = lambda x: -(-x // 8) * 8
    sums = lambda rows, lanes: F(up8(rows + 2), lanes + T)
    nsem = 40 + 16 * D + 4 * W * (1 + D)
    vm = pl.BlockSpec(memory_space=pltpu.VMEM)
    a, b = pl.pallas_call(
        functools.partial(kernel, W, N),
        out_shape=(
            jax.ShapeDtypeStruct(p.shape, jnp.float32), jax.ShapeDtypeStruct(q.shape, jnp.float32),
        ),
        in_specs=[pl.BlockSpec(memory_space=pltpu.SMEM), vm, vm, vm],
        out_specs=(vm, vm),
        scratch_shapes=[
            F(2, R + 4, K, C + T), F(2, r + 4, K, c + T), F(2, r + 4, K, c + T),
            F(R + 2, K, C + T), F(r + 2, K, c + T), F(5, K, max(C, c) + T),
            F(2, K, T), F(1, K, T), F(D, 3, 2, K, T), F(D, 3, 1, K, T),
            sums(R, C), sums(R, C), sums(r, c), sums(r, c), sums(r, c), sums(r, c),
            F(2, 2, 2, K, C), F(2, 2, K, T), F(W, 2, K, C), F(W, 2, K, C), F(D, W, K, T), F(D, W, K, T),
            F(W * (r // 2), 2, K, C),
            pltpu.SemaphoreType.DMA((nsem,)), pltpu.SemaphoreType.DMA((nsem,)),
        ],
        compiler_params=pltpu.CompilerParams(
            collective_id=0, has_side_effects=True, vmem_limit_bytes=48 * 1024 * 1024,
        ),
    )(nest_anchor, cf, p, q)
    return jnp.swapaxes(a, 1, 2), jnp.swapaxes(b, 1, 2)


def solution(mesh):
    state = P(None, "lev", ("groups", "wide"), "narrow")
    return jax.shard_map(
        functools.partial(shards, mesh.shape["wide"], mesh.shape["narrow"]),
        mesh=mesh,
        in_specs=(state, state) + (P("lev"),) * 5 + (P("groups"),),
        out_specs=(state, state),
        check_vma=False,
    )
```

```python
import functools
import jax
import jax.numpy as jnp
from jax import lax
from jax.experimental import pallas as pl
from jax.experimental.pallas import tpu as pltpu
from jax.sharding import PartitionSpec as P

T = 128


def roll(x, shift):
    return pltpu.roll(x, shift, axis=1)


def kernel(
    W, N, anchor_ref, cf_ref, p_ref, n_ref, po_ref, no_ref,
    pe, ne, ne2, lp, ln, cb, pack, pack2, cr, cr2,
    psp, prp, psn, prn, psm, prm, pick, tips, slots0, slots1, corners0, corners1, cg, ssem, rsem,
):
    R, K, C = p_ref.shape[1:]
    r, c = n_ref.shape[1], n_ref.shape[3]
    half = r // 2
    slots, corners = (slots0, slots1), (corners0, corners1)
    band = half * W
    w, n, lev = lax.axis_index("wide"), lax.axis_index("narrow"), lax.axis_index("lev")
    anchor = anchor_ref[0]
    steps = (1,) if N == 2 else (1, N - 1)
    other = {"lev": 1 - lev}
    lane = lax.broadcasted_iota(jnp.int32, (K, T), 1)

    barrier = pltpu.get_barrier_semaphore()
    count = 0
    for dw in range(W):
        for dn in (0,) + steps:
            if dw or dn:
                pl.semaphore_signal(
                    barrier, inc=1, device_id_type=pl.DeviceIdType.MESH,
                    device_id={"wide": lax.rem(w + dw, W), "narrow": lax.rem(n + dn, N)},
                )
                count += 1
    pl.semaphore_signal(barrier, inc=1, device_id=other, device_id_type=pl.DeviceIdType.MESH)

    next_send, next_recv, pending = [0], [0], []

    def take(many=1):
        next_recv[0] += many
        return next_recv[0] - many

    def guarded(cond, act):
        if cond is None:
            act()
        else:
            pl.when(cond)(act)

    def send(src, dst, sem, device, cond=None):
        copy = pltpu.make_async_remote_copy(
            src_ref=src, dst_ref=dst, send_sem=ssem.at[next_send[0]], recv_sem=rsem.at[sem],
            device_id=device, device_id_type=pl.DeviceIdType.MESH,
        )
        next_send[0] += 1
        guarded(cond, lambda: copy.start())
        pending.append((copy, cond))

    def receive(dst, sem, cond=None):
        copy = pltpu.make_async_remote_copy(
            src_ref=dst, dst_ref=dst, send_sem=ssem.at[0], recv_sem=rsem.at[sem],
            device_id=other, device_id_type=pl.DeviceIdType.MESH,
        )
        guarded(cond, lambda: copy.wait_recv())

    above, below = w > 0, w < W - 1
    up, down = {"wide": w - 1}, {"wide": w + 1}
    waits = []

    def send_rows(src, start, dst, rows, lanes):
        s = take(4)
        at = lambda ref, f, i, m: ref.at[f, pl.ds(i, m), :, pl.ds(0, lanes)]
        for f, m, k in ((0, 2, 0), (1, 1, 1)):
            send(at(src, f, start + rows - m, m), at(dst, f, 2 - m, m), s + k, down, below)
            send(at(src, f, start, m), at(dst, f, rows + 2, m), s + 2 + k, up, above)

        def wait():
            for f, m, k in ((0, 2, 0), (1, 1, 1)):
                receive(at(dst, f, 2 - m, m), s + k, above)
                receive(at(dst, f, rows + 2, m), s + 2 + k, below)
        return wait

    def send_packs(src, dst, first):
        todo = []
        for d, dn in enumerate(steps):
            to = lax.rem(n + dn, N)
            s = take(3)
            send(src, dst.at[d, 1], s + 1, {"narrow": to})
            tip = src.at[pl.ds(first, 1)]
            send(tip, dst.at[d, 0, pl.ds(first, 1)], s, {"wide": w + 1, "narrow": to}, below)
            send(tip, dst.at[d, 2, pl.ds(first, 1)], s + 2, {"wide": w - 1, "narrow": to}, above)
            todo.append((dst.at[d, 1], s + 1, None))
            todo.append((dst.at[d, 0, pl.ds(first, 1)], s, above))
            todo.append((dst.at[d, 2, pl.ds(first, 1)], s + 2, below))
        return lambda: [receive(*one) for one in todo]

    def merged(dst, at, tile, even):
        if N == 2:
            return dst[0, at, tile]
        return jnp.where(even, dst[0, at, tile], dst[1, at, tile])

    def ends(value, lanes):
        return jnp.where(lane < T // 2, value[:, :T], value[:, lanes - T:lanes])

    def send_picks(source, k):
        s = take(W)
        sems = [take(W) for _ in steps]
        for e, (row, target, cond) in enumerate((
            (anchor - 1, 0, w != 0), (anchor + band, W - 1, w != W - 1),
        )):
            local = jnp.clip(row - w * R, 0, R - 1)
            for f in range(2):
                pick[k, e, f] = source[f, local]
            tips[k, e] = ends(pick[k, e, 0], C)
            send(pick.at[k, e], slots[k].at[w], s + w, {"wide": target}, cond)
            for d, dn in enumerate(steps):
                send(
                    tips.at[k, e], corners[k].at[d, w], sems[d] + w,
                    {"wide": target, "narrow": lax.rem(n + dn, N)}, cond,
                )
        for e, target in ((0, 0), (1, W - 1)):
            for d, dn in enumerate(steps):
                send(
                    tips.at[k, e], corners[k].at[d, w], sems[d] + w,
                    {"narrow": lax.rem(n + dn, N)}, w == target,
                )

            def keep(e=e):
                slots[k][w] = pick[k, e]
            pl.when(w == target)(keep)

        def wait():
            for target in (0, W - 1):
                for src in range(W):
                    if src != target:
                        receive(slots[k].at[src], s + src, w == target)
                    for d in range(len(steps)):
                        receive(corners[k].at[d, src], sems[d] + src, w == target)
        return wait

    def set_edges(dst, ks):
        scale = 1.0 / len(ks)
        wider = (
            lax.broadcasted_iota(jnp.int32, (C, c), 1) // 2
            == lax.broadcasted_iota(jnp.int32, (C, c), 0)
        ).astype(jnp.float32)
        for row, target, first, near in (
            (anchor - 1, 0, 0, 1), (anchor + band, W - 1, r + 2, r + 2),
        ):
            owner = lax.div(row, R)

            def fill(owner=owner, first=first, near=near):
                for f in range(2):
                    value = scale * sum(slots[k][owner, f] for k in ks)
                    fine = jnp.dot(
                        value, wider, precision=lax.Precision.HIGHEST,
                        preferred_element_type=jnp.float32,
                    )
                    dst[f, first, :, 0:c] = fine
                    dst[f, first + 1, :, 0:c] = fine
                left = scale * sum(corners[k][0, owner] for k in ks)
                if N > 2:
                    right = scale * sum(corners[k][1, owner] for k in ks)
                    left = jnp.where(lane < T // 2, right, left)
                dst[0, near, :, c:c + T] = left
            pl.when(w == target)(fill)

    def column_sums(ext, rows, out):
        weights = cb[0, :, 0:ext.shape[3]]

        def body(j, _):
            out[pl.ds(j, 1), :] = jnp.sum(weights * ext[0, j + 1], axis=0, keepdims=True)
            return 0
        lax.fori_loop(0, rows + 2, body, 0, unroll=True)

    def advance(ext, rows, lanes, mine, theirs, lap, f, g, store):
        L = lanes + T
        near = lambda x: roll(x, 1) + roll(x, L - 1)

        def inner(j, _):
            x = ext[0, j + 1]
            lap[j] = ext[0, j + 2] + ext[0, j] + near(x) - 4.0 * x
            return 0
        lax.fori_loop(0, rows + 2, inner, 0, unroll=True)
        diffuse, smooth = f * cb[1, :, 0:lanes], g * cb[2, :, 0:lanes]
        couple, advect = f * cb[3, :, 0:lanes], f * cb[4, :, 0:lanes]

        def body(i, _):
            total = lambda j: mine[pl.ds(j, 1), :] + theirs[pl.ds(j, 1), :]
            p0, p1, p2 = total(i), total(i + 1), total(i + 2)
            wide1 = jnp.broadcast_to(p1, (8, L))
            pl_, pr = roll(wide1, 1)[0:1, :lanes], roll(wide1, L - 1)[0:1, :lanes]
            p0, p1, p2 = p0[:, :lanes], p1[:, :lanes], p2[:, :lanes]
            lap_p = p2 + p0 + pr + pl_ - 4.0 * p1
            drp, dcp = 0.5 * (p2 - p0), 0.5 * (pr - pl_)
            l1 = lap[i + 1]
            m1 = l1[:, :lanes]
            lap2 = lap[i + 2][:, :lanes] + lap[i][:, :lanes] + near(l1)[:, :lanes] - 4.0 * m1
            h = ext[0, i + 2][:, :lanes]
            store(0, i, h + diffuse * m1 - smooth * lap2 + couple * lap_p)
            q = ext[1, i + 2]
            qu, qd, q1 = ext[1, i + 1][:, :lanes], ext[1, i + 3][:, :lanes], q[:, :lanes]
            ql, qr = roll(q, 1)[:, :lanes], roll(q, L - 1)[:, :lanes]
            lap_q = qd + qu + qr + ql - 4.0 * q1
            drift = drp * (0.5 * (qd - qu)) + dcp * (0.5 * (qr - ql))
            store(1, i, q1 + diffuse * lap_q - advect * drift)
            return 0
        lax.fori_loop(0, rows, body, 0, unroll=True)

    def pack_nest(ref, start, dst, tile):
        dst[tile] = jnp.zeros((K, T), jnp.float32)

        def body(i, _):
            for f in range(2):
                slot = f * r + i
                x = ends(ref[f, i + start], c)
                dst[tile] = jnp.where(lane // 4 == slot, roll(x, 4 * slot + 2), dst[tile])
            return 0
        lax.fori_loop(0, r, body, 0, unroll=True)

    pl.semaphore_wait(barrier, count + 1)
    wait_rows = [send_rows(p_ref, 0, pe, R, C), send_rows(n_ref, 0, ne, r, c)]
    wait_old = send_picks(p_ref, 0)
    pack[0] = jnp.zeros((K, T), jnp.float32)

    def pack_parent(i, _):
        for f in range(2):
            slot = f * R + i
            x = ends(p_ref[f, i], C)
            pack[0] = jnp.where(lane // 4 == slot, roll(x, 4 * slot + 2), pack[0])
        return 0
    lax.fori_loop(0, R, pack_parent, 0, unroll=True)
    pack_nest(n_ref, 0, pack, 1)
    for slot, row in ((2 * r, 0), (2 * r + 1, R - 1)):
        x = ends(p_ref[0, row], C)
        pack[1] = jnp.where(lane // 4 == slot, roll(x, 4 * slot + 2), pack[1])
    wait_packs = send_packs(pack, cr, 1)

    for j in range(5):
        cb[j] = jnp.broadcast_to(cf_ref[:, j:j + 1], cb.shape[1:])
    for f in range(2):
        pe[f, 2:R + 2, :, 0:C] = p_ref[f]
        ne[f, 2:r + 2, :, 0:c] = n_ref[f]
    for cond, first in ((w == 0, 0), (w == W - 1, R + 2)):
        def clear(first=first):
            pe[:, first:first + 2] = jnp.zeros((2, 2, K, C + T), jnp.float32)
        pl.when(cond)(clear)
    left_part = lane % 4 < 2
    side = lambda slot: lax.rem(2 * T - 2 - 4 * slot, T)
    wait_packs()
    m0 = merged(cr, 1, 0, left_part)
    m1 = merged(cr, 1, 1, left_part)

    def unpack_parent(i, _):
        for f in range(2):
            pe[f, i + 2, :, C:C + T] = roll(m0, side(f * R + i))
        return 0
    lax.fori_loop(0, R, unpack_parent, 0, unroll=True)

    def unpack_nest(dst, m):
        def body(i, _):
            for f in range(2):
                dst[f, i + 2, :, c:c + T] = roll(m, side(f * r + i))
            return 0
        lax.fori_loop(0, r, body, 0, unroll=True)
    unpack_nest(ne, m1)

    @pl.when(above)
    def _():
        m = merged(cr, 0, 1, left_part)
        pe[0, 1, :, C:C + T] = roll(m, side(2 * r + 1))
        ne[0, 1, :, c:c + T] = roll(m, side(r - 1))

    @pl.when(below)
    def _():
        m = merged(cr, 2, 1, left_part)
        pe[0, R + 2, :, C:C + T] = roll(m, side(2 * r))
        ne[0, r + 2, :, c:c + T] = roll(m, side(0))

    def share(mine, theirs):
        s = take()
        send(mine, theirs, s, other)
        return lambda: receive(theirs, s)

    wait_rows[0]()
    column_sums(pe, R, psp)
    wait_p = share(psp, prp)
    wait_rows[1]()
    wait_old()
    set_edges(ne, (0,))
    column_sums(ne, r, psn)
    wait_n = share(psn, prn)
    wait_p()

    def store_parent(f, i, v):
        po_ref[f, i] = v

    def store_mid(f, i, v):
        ne2[f, i + 2, :, 0:c] = v

    def store_nest(f, i, v):
        no_ref[f, i] = v

    advance(pe, R, C, psp, prp, lp, 1.0, 1.0, store_parent)
    wait_new = send_picks(po_ref, 1)
    wait_n()
    advance(ne, r, c, psn, prn, ln, 2.0, 8.0, store_mid)
    wait_mid = send_rows(ne2, 2, ne2, r, c)
    pack_nest(ne2, 2, pack2, 0)
    wait_packs2 = send_packs(pack2, cr2, 0)
    wait_new()
    set_edges(ne2, (0, 1))
    wait_packs2()
    unpack_nest(ne2, merged(cr2, 1, 0, left_part))

    @pl.when(above)
    def _():
        ne2[0, 1, :, c:c + T] = roll(merged(cr2, 0, 0, left_part), side(r - 1))

    @pl.when(below)
    def _():
        ne2[0, r + 2, :, c:c + T] = roll(merged(cr2, 2, 0, left_part), side(0))

    wait_mid()
    column_sums(ne2, r, psm)
    wait_m = share(psm, prm)
    wait_m()
    advance(ne2, r, c, psm, prm, ln, 2.0, 8.0, store_nest)
    narrower = jnp.where(
        lax.broadcasted_iota(jnp.int32, (c, C), 0) // 2
        == lax.broadcasted_iota(jnp.int32, (c, C), 1), 0.25, 0.0
    )
    base = w * half
    for i in range(half):
        for f in range(2):
            cg[base + i, f] = jnp.dot(
                no_ref[f, 2 * i] + no_ref[f, 2 * i + 1], narrower,
                precision=lax.Precision.HIGHEST, preferred_element_type=jnp.float32,
            )
    s = take(W)
    for dw in range(1, W):
        block = cg.at[pl.ds(base, half)]
        send(block, block, s + w, {"wide": lax.rem(w + dw, W)})
    for dw in range(1, W):
        src = lax.rem(w + dw, W)
        receive(cg.at[pl.ds(src * half, half)], s + src)

    def absorb(i, _):
        at = w * R + i - anchor
        inside = (at >= 0) & (at < band)
        piece = jnp.clip(at, 0, band - 1)
        for f in range(2):
            po_ref[f, i] = jnp.where(inside, cg[piece, f], po_ref[f, i])
        return 0
    lax.fori_loop(0, R, absorb, 0, unroll=True)
    for copy, cond in pending:
        guarded(cond, lambda copy=copy: copy.wait_send())


def shards(
    W, N, parent_state, nest_state, level_weights, diffusion, smoothing, coupling, transport, nest_anchor
):
    p = jnp.swapaxes(parent_state, 1, 2)
    q = jnp.swapaxes(nest_state, 1, 2)
    cf = jnp.stack([level_weights, diffusion, smoothing, coupling, transport], axis=1)
    _, R, K, C = p.shape
    r, c = q.shape[1], q.shape[3]
    D = 1 if N == 2 else 2
    F = lambda *dims: pltpu.VMEM(dims, jnp.float32)
    up8 = lambda x: -(-x // 8) * 8
    sums = lambda rows, lanes: F(up8(rows + 2), lanes + T)
    nsem = 40 + 16 * D + 4 * W * (1 + D)
    vm = pl.BlockSpec(memory_space=pltpu.VMEM)
    a, b = pl.pallas_call(
        functools.partial(kernel, W, N),
        out_shape=(
            jax.ShapeDtypeStruct(p.shape, jnp.float32), jax.ShapeDtypeStruct(q.shape, jnp.float32),
        ),
        in_specs=[pl.BlockSpec(memory_space=pltpu.SMEM), vm, vm, vm],
        out_specs=(vm, vm),
        scratch_shapes=[
            F(2, R + 4, K, C + T), F(2, r + 4, K, c + T), F(2, r + 4, K, c + T),
            F(R + 2, K, C + T), F(r + 2, K, c + T), F(5, K, max(C, c) + T),
            F(2, K, T), F(1, K, T), F(D, 3, 2, K, T), F(D, 3, 1, K, T),
            sums(R, C), sums(R, C), sums(r, c), sums(r, c), sums(r, c), sums(r, c),
            F(2, 2, 2, K, C), F(2, 2, K, T), F(W, 2, K, C), F(W, 2, K, C), F(D, W, K, T), F(D, W, K, T),
            F(W * (r // 2), 2, K, C),
            pltpu.SemaphoreType.DMA((nsem,)), pltpu.SemaphoreType.DMA((nsem,)),
        ],
        compiler_params=pltpu.CompilerParams(
            collective_id=0, has_side_effects=True, vmem_limit_bytes=48 * 1024 * 1024,
        ),
    )(nest_anchor, cf, p, q)
    return jnp.swapaxes(a, 1, 2), jnp.swapaxes(b, 1, 2)


def solution(mesh):
    state = P(None, "lev", ("groups", "wide"), "narrow")
    return jax.shard_map(
        functools.partial(shards, mesh.shape["wide"], mesh.shape["narrow"]),
        mesh=mesh,
        in_specs=(state, state) + (P("lev"),) * 5 + (P("groups"),),
        out_specs=(state, state),
        check_vma=False,
    )
```

```python
import functools
import jax
import jax.numpy as jnp
from jax import lax
from jax.experimental import pallas as pl
from jax.experimental.pallas import tpu as pltpu
from jax.sharding import PartitionSpec as P

T = 128


def roll(x, shift):
    return pltpu.roll(x, shift, axis=1)


def kernel(
    W, N, anchor_ref, cf_ref, p_ref, n_ref, po_ref, no_ref,
    pe, ne, ne2, lp, ln, cb, pack, pack2, cr, cr2,
    psp, prp, psn, prn, psm, prm, pick, tips, slots0, slots1, corners0, corners1, cg, ssem, rsem,
):
    R, K, C = p_ref.shape[1:]
    r, c = n_ref.shape[1], n_ref.shape[3]
    half = r // 2
    slots, corners = (slots0, slots1), (corners0, corners1)
    band = half * W
    w, n, lev = lax.axis_index("wide"), lax.axis_index("narrow"), lax.axis_index("lev")
    anchor = anchor_ref[0]
    steps = (1,) if N == 2 else (1, N - 1)
    other = {"lev": 1 - lev}
    lane = lax.broadcasted_iota(jnp.int32, (K, T), 1)

    barrier = pltpu.get_barrier_semaphore()
    count = 0
    for dw in range(W):
        for dn in (0,) + steps:
            if dw or dn:
                pl.semaphore_signal(
                    barrier, inc=1, device_id_type=pl.DeviceIdType.MESH,
                    device_id={"wide": lax.rem(w + dw, W), "narrow": lax.rem(n + dn, N)},
                )
                count += 1
    pl.semaphore_signal(barrier, inc=1, device_id=other, device_id_type=pl.DeviceIdType.MESH)

    next_send, next_recv, pending = [0], [0], []

    def take(many=1):
        next_recv[0] += many
        return next_recv[0] - many

    def guarded(cond, act):
        if cond is None:
            act()
        else:
            pl.when(cond)(act)

    def send(src, dst, sem, device, cond=None):
        copy = pltpu.make_async_remote_copy(
            src_ref=src, dst_ref=dst, send_sem=ssem.at[next_send[0]], recv_sem=rsem.at[sem],
            device_id=device, device_id_type=pl.DeviceIdType.MESH,
        )
        next_send[0] += 1
        guarded(cond, lambda: copy.start())
        pending.append((copy, cond))

    def receive(dst, sem, cond=None):
        copy = pltpu.make_async_remote_copy(
            src_ref=dst, dst_ref=dst, send_sem=ssem.at[0], recv_sem=rsem.at[sem],
            device_id=other, device_id_type=pl.DeviceIdType.MESH,
        )
        guarded(cond, lambda: copy.wait_recv())

    above, below = w > 0, w < W - 1
    up, down = {"wide": w - 1}, {"wide": w + 1}
    waits = []

    def send_rows(src, start, dst, rows, lanes):
        s = take(4)
        at = lambda ref, f, i, m: ref.at[f, pl.ds(i, m), :, pl.ds(0, lanes)]
        for f, m, k in ((0, 2, 0), (1, 1, 1)):
            send(at(src, f, start + rows - m, m), at(dst, f, 2 - m, m), s + k, down, below)
            send(at(src, f, start, m), at(dst, f, rows + 2, m), s + 2 + k, up, above)

        def wait():
            for f, m, k in ((0, 2, 0), (1, 1, 1)):
                receive(at(dst, f, 2 - m, m), s + k, above)
                receive(at(dst, f, rows + 2, m), s + 2 + k, below)
        return wait

    def send_packs(src, dst, first):
        todo = []
        for d, dn in enumerate(steps):
            to = lax.rem(n + dn, N)
            s = take(3)
            send(src, dst.at[d, 1], s + 1, {"narrow": to})
            tip = src.at[pl.ds(first, 1)]
            send(tip, dst.at[d, 0, pl.ds(first, 1)], s, {"wide": w + 1, "narrow": to}, below)
            send(tip, dst.at[d, 2, pl.ds(first, 1)], s + 2, {"wide": w - 1, "narrow": to}, above)
            todo.append((dst.at[d, 1], s + 1, None))
            todo.append((dst.at[d, 0, pl.ds(first, 1)], s, above))
            todo.append((dst.at[d, 2, pl.ds(first, 1)], s + 2, below))
        return lambda: [receive(*one) for one in todo]

    def merged(dst, at, tile, even):
        if N == 2:
            return dst[0, at, tile]
        return jnp.where(even, dst[0, at, tile], dst[1, at, tile])

    def ends(value, lanes):
        return jnp.where(lane < T // 2, value[:, :T], value[:, lanes - T:lanes])

    def send_picks(source, k):
        s = take(W)
        sems = [take(W) for _ in steps]
        for e, (row, target, cond) in enumerate((
            (anchor - 1, 0, w != 0), (anchor + band, W - 1, w != W - 1),
        )):
            local = jnp.clip(row - w * R, 0, R - 1)
            for f in range(2):
                pick[k, e, f] = source[f, local]
            x = ends(pick[k, e, 0], C)
            folded = jnp.zeros((8, T), jnp.float32)
            for part in range(K // 8):
                turned = roll(x[8 * part:8 * part + 8], 2 * part + 1)
                folded = jnp.where(lane[:8] // 2 == part, turned, folded)
            tips[k, e] = folded
            send(pick.at[k, e], slots[k].at[w], s + w, {"wide": target}, cond)
            for d, dn in enumerate(steps):
                send(
                    tips.at[k, e], corners[k].at[d, w], sems[d] + w,
                    {"wide": target, "narrow": lax.rem(n + dn, N)}, cond,
                )
        for e, target in ((0, 0), (1, W - 1)):
            for d, dn in enumerate(steps):
                send(
                    tips.at[k, e], corners[k].at[d, w], sems[d] + w,
                    {"narrow": lax.rem(n + dn, N)}, w == target,
                )

            def keep(e=e):
                slots[k][w] = pick[k, e]
            pl.when(w == target)(keep)

        def wait():
            for target in (0, W - 1):
                for src in range(W):
                    if src != target:
                        receive(slots[k].at[src], s + src, w == target)
                    for d in range(len(steps)):
                        receive(corners[k].at[d, src], sems[d] + src, w == target)
        return wait

    def set_edges(dst, ks):
        scale = 1.0 / len(ks)
        wider = (
            lax.broadcasted_iota(jnp.int32, (C, c), 1) // 2
            == lax.broadcasted_iota(jnp.int32, (C, c), 0)
        ).astype(jnp.float32)
        for row, target, first, near in (
            (anchor - 1, 0, 0, 1), (anchor + band, W - 1, r + 2, r + 2),
        ):
            owner = lax.div(row, R)

            def fill(owner=owner, first=first, near=near):
                for f in range(2):
                    value = scale * sum(slots[k][owner, f] for k in ks)
                    fine = jnp.dot(
                        value, wider, precision=lax.Precision.HIGHEST,
                        preferred_element_type=jnp.float32,
                    )
                    dst[f, first, :, 0:c] = fine
                    dst[f, first + 1, :, 0:c] = fine
                left = scale * sum(corners[k][0, owner] for k in ks)
                if N > 2:
                    right = scale * sum(corners[k][1, owner] for k in ks)
                    left = jnp.where(lane[:8] % 2 == 0, left, right)
                for part in range(K // 8):
                    dst[0, near, 8 * part:8 * part + 8, c:c + T] = roll(left, T - 1 - 2 * part)
            pl.when(w == target)(fill)

    def column_sums(ext, rows, out):
        weights = cb[0, :, 0:ext.shape[3]]

        def body(j, _):
            out[pl.ds(j, 1), :] = jnp.sum(weights * ext[0, j + 1], axis=0, keepdims=True)
            return 0
        lax.fori_loop(0, rows + 2, body, 0, unroll=True)

    def advance(ext, rows, lanes, mine, theirs, lap, f, g, store, parts=1, after=None):
        L = lanes + T
        near = lambda x: roll(x, 1) + roll(x, L - 1)

        def inner(j, _):
            x = ext[0, j + 1]
            lap[j] = ext[0, j + 2] + ext[0, j] + near(x) - 4.0 * x
            return 0
        lax.fori_loop(0, rows + 2, inner, 0, unroll=True)
        diffuse, smooth = f * cb[1, :, 0:lanes], g * cb[2, :, 0:lanes]
        couple, advect = f * cb[3, :, 0:lanes], f * cb[4, :, 0:lanes]

        def body(i, _):
            total = lambda j: mine[pl.ds(j, 1), :] + theirs[pl.ds(j, 1), :]
            p0, p1, p2 = total(i), total(i + 1), total(i + 2)
            wide1 = jnp.broadcast_to(p1, (8, L))
            pl_, pr = roll(wide1, 1)[0:1, :lanes], roll(wide1, L - 1)[0:1, :lanes]
            p0, p1, p2 = p0[:, :lanes], p1[:, :lanes], p2[:, :lanes]
            lap_p = p2 + p0 + pr + pl_ - 4.0 * p1
            drp, dcp = 0.5 * (p2 - p0), 0.5 * (pr - pl_)
            l1 = lap[i + 1]
            m1 = l1[:, :lanes]
            lap2 = lap[i + 2][:, :lanes] + lap[i][:, :lanes] + near(l1)[:, :lanes] - 4.0 * m1
            h = ext[0, i + 2][:, :lanes]
            store(0, i, h + diffuse * m1 - smooth * lap2 + couple * lap_p)
            q = ext[1, i + 2]
            qu, qd, q1 = ext[1, i + 1][:, :lanes], ext[1, i + 3][:, :lanes], q[:, :lanes]
            ql, qr = roll(q, 1)[:, :lanes], roll(q, L - 1)[:, :lanes]
            lap_q = qd + qu + qr + ql - 4.0 * q1
            drift = drp * (0.5 * (qd - qu)) + dcp * (0.5 * (qr - ql))
            store(1, i, q1 + diffuse * lap_q - advect * drift)
            return 0
        size = rows // parts
        for part in range(parts):
            lax.fori_loop(part * size, (part + 1) * size, body, 0, unroll=True)
            if after:
                after(part)

    def pack_nest(ref, start, dst, tile):
        dst[tile] = jnp.zeros((K, T), jnp.float32)

        def body(i, _):
            for f in range(2):
                slot = f * r + i
                x = ends(ref[f, i + start], c)
                dst[tile] = jnp.where(lane // 4 == slot, roll(x, 4 * slot + 2), dst[tile])
            return 0
        lax.fori_loop(0, r, body, 0, unroll=True)

    pl.semaphore_wait(barrier, count + 1)
    wait_rows = [send_rows(p_ref, 0, pe, R, C), send_rows(n_ref, 0, ne, r, c)]
    pack[0] = jnp.zeros((K, T), jnp.float32)

    def pack_parent(i, _):
        for f in range(2):
            slot = f * R + i
            x = ends(p_ref[f, i], C)
            pack[0] = jnp.where(lane // 4 == slot, roll(x, 4 * slot + 2), pack[0])
        return 0
    lax.fori_loop(0, R, pack_parent, 0, unroll=True)
    pack_nest(n_ref, 0, pack, 1)
    for slot, row in ((2 * r, 0), (2 * r + 1, R - 1)):
        x = ends(p_ref[0, row], C)
        pack[1] = jnp.where(lane // 4 == slot, roll(x, 4 * slot + 2), pack[1])
    wait_packs = send_packs(pack, cr, 1)
    wait_old = send_picks(p_ref, 0)

    for j in range(5):
        cb[j] = jnp.broadcast_to(cf_ref[:, j:j + 1], cb.shape[1:])
    for f in range(2):
        pe[f, 2:R + 2, :, 0:C] = p_ref[f]
        ne[f, 2:r + 2, :, 0:c] = n_ref[f]
    for cond, first in ((w == 0, 0), (w == W - 1, R + 2)):
        def clear(first=first):
            pe[:, first:first + 2] = jnp.zeros((2, 2, K, C + T), jnp.float32)
        pl.when(cond)(clear)
    left_part = lane % 4 < 2
    side = lambda slot: lax.rem(2 * T - 2 - 4 * slot, T)
    wait_packs()
    m0 = merged(cr, 1, 0, left_part)
    m1 = merged(cr, 1, 1, left_part)

    def unpack_parent(i, _):
        for f in range(2):
            pe[f, i + 2, :, C:C + T] = roll(m0, side(f * R + i))
        return 0
    lax.fori_loop(0, R, unpack_parent, 0, unroll=True)

    def unpack_nest(dst, m):
        def body(i, _):
            for f in range(2):
                dst[f, i + 2, :, c:c + T] = roll(m, side(f * r + i))
            return 0
        lax.fori_loop(0, r, body, 0, unroll=True)
    unpack_nest(ne, m1)

    @pl.when(above)
    def _():
        m = merged(cr, 0, 1, left_part)
        pe[0, 1, :, C:C + T] = roll(m, side(2 * r + 1))
        ne[0, 1, :, c:c + T] = roll(m, side(r - 1))

    @pl.when(below)
    def _():
        m = merged(cr, 2, 1, left_part)
        pe[0, R + 2, :, C:C + T] = roll(m, side(2 * r))
        ne[0, r + 2, :, c:c + T] = roll(m, side(0))

    def share(mine, theirs):
        s = take()
        send(mine, theirs, s, other)
        return lambda: receive(theirs, s)

    wait_rows[0]()
    column_sums(pe, R, psp)
    wait_p = share(psp, prp)
    wait_rows[1]()
    wait_old()
    set_edges(ne, (0,))
    column_sums(ne, r, psn)
    wait_n = share(psn, prn)
    wait_p()

    def store_parent(f, i, v):
        po_ref[f, i] = v

    def store_mid(f, i, v):
        ne2[f, i + 2, :, 0:c] = v

    def store_nest(f, i, v):
        no_ref[f, i] = v

    advance(pe, R, C, psp, prp, lp, 1.0, 1.0, store_parent)
    wait_new = send_picks(po_ref, 1)
    wait_n()
    advance(ne, r, c, psn, prn, ln, 2.0, 8.0, store_mid)
    wait_mid = send_rows(ne2, 2, ne2, r, c)
    pack_nest(ne2, 2, pack2, 0)
    wait_packs2 = send_packs(pack2, cr2, 0)
    wait_new()
    set_edges(ne2, (0, 1))
    wait_packs2()
    unpack_nest(ne2, merged(cr2, 1, 0, left_part))

    @pl.when(above)
    def _():
        ne2[0, 1, :, c:c + T] = roll(merged(cr2, 0, 0, left_part), side(r - 1))

    @pl.when(below)
    def _():
        ne2[0, r + 2, :, c:c + T] = roll(merged(cr2, 2, 0, left_part), side(0))

    wait_mid()
    column_sums(ne2, r, psm)
    wait_m = share(psm, prm)
    wait_m()
    narrower = jnp.where(
        lax.broadcasted_iota(jnp.int32, (c, C), 0) // 2
        == lax.broadcasted_iota(jnp.int32, (c, C), 1), 0.25, 0.0
    )
    base = w * half
    pieces = 2 if half % 2 == 0 else 1
    many = half // pieces
    s_down, s_up = take(pieces * W), take(pieces * W)
    block = lambda at, piece: cg.at[pl.ds(at * half + piece * many, many)]

    def send_coarse(piece):
        for i in range(piece * many, (piece + 1) * many):
            for f in range(2):
                cg[base + i, f] = jnp.dot(
                    no_ref[f, 2 * i] + no_ref[f, 2 * i + 1], narrower,
                    precision=lax.Precision.HIGHEST, preferred_element_type=jnp.float32,
                )
        own = block(w, piece)
        for far in (2, 1):
            send(own, own, s_down + piece * W + w, {"wide": w + far}, w + far < W)
            send(own, own, s_up + piece * W + w, {"wide": w - far}, w - far >= 0)

    advance(ne2, r, c, psm, prm, ln, 2.0, 8.0, store_nest, pieces, send_coarse)
    for hop in (2, 1) + tuple(range(3, W)):
        for piece in range(pieces):
            for first, src, there, to, more in (
                (s_down, jnp.maximum(w - hop, 0), w >= hop, down, below),
                (s_up, jnp.minimum(w + hop, W - 1), w + hop < W, up, above),
            ):
                one, sem = block(src, piece), first + piece * W + src
                receive(one, sem, there)
                if 2 <= hop < W - 1:
                    send(one, one, sem, to, there & more)

    def absorb(i, _):
        at = w * R + i - anchor
        inside = (at >= 0) & (at < band)
        piece = jnp.clip(at, 0, band - 1)
        for f in range(2):
            po_ref[f, i] = jnp.where(inside, cg[piece, f], po_ref[f, i])
        return 0
    lax.fori_loop(0, R, absorb, 0, unroll=True)
    for copy, cond in pending:
        guarded(cond, lambda copy=copy: copy.wait_send())


def shards(
    W, N, parent_state, nest_state, level_weights, diffusion, smoothing, coupling, transport, nest_anchor
):
    p = jnp.swapaxes(parent_state, 1, 2)
    q = jnp.swapaxes(nest_state, 1, 2)
    cf = jnp.stack([level_weights, diffusion, smoothing, coupling, transport], axis=1)
    _, R, K, C = p.shape
    r, c = q.shape[1], q.shape[3]
    D = 1 if N == 2 else 2
    F = lambda *dims: pltpu.VMEM(dims, jnp.float32)
    up8 = lambda x: -(-x // 8) * 8
    sums = lambda rows, lanes: F(up8(rows + 2), lanes + T)
    nsem = 64 + 24 * D + 4 * W * (3 + D)
    vm = pl.BlockSpec(memory_space=pltpu.VMEM)
    a, b = pl.pallas_call(
        functools.partial(kernel, W, N),
        out_shape=(
            jax.ShapeDtypeStruct(p.shape, jnp.float32), jax.ShapeDtypeStruct(q.shape, jnp.float32),
        ),
        in_specs=[pl.BlockSpec(memory_space=pltpu.SMEM), vm, vm, vm],
        out_specs=(vm, vm),
        scratch_shapes=[
            F(2, R + 4, K, C + T), F(2, r + 4, K, c + T), F(2, r + 4, K, c + T),
            F(R + 2, K, C + T), F(r + 2, K, c + T), F(5, K, max(C, c) + T),
            F(2, K, T), F(1, K, T), F(D, 3, 2, K, T), F(D, 3, 1, K, T),
            sums(R, C), sums(R, C), sums(r, c), sums(r, c), sums(r, c), sums(r, c),
            F(2, 2, 2, K, C), F(2, 2, 8, T), F(W, 2, K, C), F(W, 2, K, C), F(D, W, 8, T), F(D, W, 8, T),
            F(W * (r // 2), 2, K, C),
            pltpu.SemaphoreType.DMA((nsem,)), pltpu.SemaphoreType.DMA((nsem,)),
        ],
        compiler_params=pltpu.CompilerParams(
            collective_id=0, has_side_effects=True, vmem_limit_bytes=48 * 1024 * 1024,
        ),
    )(nest_anchor, cf, p, q)
    return jnp.swapaxes(a, 1, 2), jnp.swapaxes(b, 1, 2)


def solution(mesh):
    state = P(None, "lev", ("groups", "wide"), "narrow")
    return jax.shard_map(
        functools.partial(shards, mesh.shape["wide"], mesh.shape["narrow"]),
        mesh=mesh,
        in_specs=(state, state) + (P("lev"),) * 5 + (P("groups"),),
        out_specs=(state, state),
        check_vma=False,
    )
```

```python
import functools
import jax
import jax.numpy as jnp
from jax import lax
from jax.experimental import pallas as pl
from jax.experimental.pallas import tpu as pltpu
from jax.sharding import PartitionSpec as P

T = 128


def roll(x, shift):
    return pltpu.roll(x, shift, axis=1)


def kernel(
    W, N, anchor_ref, cf_ref, p_ref, n_ref, po_ref, no_ref,
    pe, ne, ne2, lp, ln, cb, pack, pack2, cr, cr2,
    psp, prp, psn, prn, psm, prm, pick, tips, slots0, slots1, corners0, corners1, cg, ssem, rsem,
):
    R, K, C = p_ref.shape[1:]
    r, c = n_ref.shape[1], n_ref.shape[3]
    half = r // 2
    slots, corners = (slots0, slots1), (corners0, corners1)
    band = half * W
    w, n, lev = lax.axis_index("wide"), lax.axis_index("narrow"), lax.axis_index("lev")
    anchor = anchor_ref[0]
    steps = (1,) if N == 2 else (1, N - 1)
    other = {"lev": 1 - lev}
    lane = lax.broadcasted_iota(jnp.int32, (K, T), 1)

    barrier = pltpu.get_barrier_semaphore()
    count = 0
    for dw in range(W):
        for dn in (0,) + steps:
            if dw or dn:
                pl.semaphore_signal(
                    barrier, inc=1, device_id_type=pl.DeviceIdType.MESH,
                    device_id={"wide": lax.rem(w + dw, W), "narrow": lax.rem(n + dn, N)},
                )
                count += 1
    pl.semaphore_signal(barrier, inc=1, device_id=other, device_id_type=pl.DeviceIdType.MESH)

    next_send, next_recv, pending = [0], [0], []

    def take(many=1):
        next_recv[0] += many
        return next_recv[0] - many

    def guarded(cond, act):
        if cond is None:
            act()
        else:
            pl.when(cond)(act)

    def send(src, dst, sem, device, cond=None):
        copy = pltpu.make_async_remote_copy(
            src_ref=src, dst_ref=dst, send_sem=ssem.at[next_send[0]], recv_sem=rsem.at[sem],
            device_id=device, device_id_type=pl.DeviceIdType.MESH,
        )
        next_send[0] += 1
        guarded(cond, lambda: copy.start())
        pending.append((copy, cond))

    def receive(dst, sem, cond=None):
        copy = pltpu.make_async_remote_copy(
            src_ref=dst, dst_ref=dst, send_sem=ssem.at[0], recv_sem=rsem.at[sem],
            device_id=other, device_id_type=pl.DeviceIdType.MESH,
        )
        guarded(cond, lambda: copy.wait_recv())

    above, below = w > 0, w < W - 1
    up, down = {"wide": w - 1}, {"wide": w + 1}
    waits = []

    def send_rows(src, start, dst, rows, lanes):
        s = take(4)
        at = lambda ref, f, i, m: ref.at[f, pl.ds(i, m), :, pl.ds(0, lanes)]
        for f, m, k in ((0, 2, 0), (1, 1, 1)):
            send(at(src, f, start + rows - m, m), at(dst, f, 2 - m, m), s + k, down, below)
            send(at(src, f, start, m), at(dst, f, rows + 2, m), s + 2 + k, up, above)

        def wait():
            for f, m, k in ((0, 2, 0), (1, 1, 1)):
                receive(at(dst, f, 2 - m, m), s + k, above)
                receive(at(dst, f, rows + 2, m), s + 2 + k, below)
        return wait

    def send_packs(src, dst, first):
        todo = []
        for d, dn in enumerate(steps):
            to = lax.rem(n + dn, N)
            s = take(3)
            send(src, dst.at[d, 1], s + 1, {"narrow": to})
            tip = src.at[pl.ds(first, 1)]
            send(tip, dst.at[d, 0, pl.ds(first, 1)], s, {"wide": w + 1, "narrow": to}, below)
            send(tip, dst.at[d, 2, pl.ds(first, 1)], s + 2, {"wide": w - 1, "narrow": to}, above)
            todo.append((dst.at[d, 1], s + 1, None))
            todo.append((dst.at[d, 0, pl.ds(first, 1)], s, above))
            todo.append((dst.at[d, 2, pl.ds(first, 1)], s + 2, below))
        return lambda: [receive(*one) for one in todo]

    def merged(dst, at, tile, even):
        if N == 2:
            return dst[0, at, tile]
        return jnp.where(even, dst[0, at, tile], dst[1, at, tile])

    def ends(value, lanes):
        return jnp.where(lane < T // 2, value[:, :T], value[:, lanes - T:lanes])

    def send_picks(source, k):
        s = take(W)
        sems = [take(W) for _ in steps]
        for e, (row, target, cond) in enumerate((
            (anchor - 1, 0, w != 0), (anchor + band, W - 1, w != W - 1),
        )):
            local = jnp.clip(row - w * R, 0, R - 1)
            for f in range(2):
                pick[k, e, f] = source[f, local]
            x = ends(pick[k, e, 0], C)
            folded = jnp.zeros((8, T), jnp.float32)
            for part in range(K // 8):
                turned = roll(x[8 * part:8 * part + 8], 2 * part + 1)
                folded = jnp.where(lane[:8] // 2 == part, turned, folded)
            tips[k, e] = folded
            send(pick.at[k, e], slots[k].at[w], s + w, {"wide": target}, cond)
            for d, dn in enumerate(steps):
                send(
                    tips.at[k, e], corners[k].at[d, w], sems[d] + w,
                    {"wide": target, "narrow": lax.rem(n + dn, N)}, cond,
                )
        for e, target in ((0, 0), (1, W - 1)):
            for d, dn in enumerate(steps):
                send(
                    tips.at[k, e], corners[k].at[d, w], sems[d] + w,
                    {"narrow": lax.rem(n + dn, N)}, w == target,
                )

            def keep(e=e):
                slots[k][w] = pick[k, e]
            pl.when(w == target)(keep)

        def wait():
            for target in (0, W - 1):
                for src in range(W):
                    if src != target:
                        receive(slots[k].at[src], s + src, w == target)
                    for d in range(len(steps)):
                        receive(corners[k].at[d, src], sems[d] + src, w == target)
        return wait

    def set_edges(dst, ks):
        scale = 1.0 / len(ks)
        wider = (
            lax.broadcasted_iota(jnp.int32, (C, c), 1) // 2
            == lax.broadcasted_iota(jnp.int32, (C, c), 0)
        ).astype(jnp.float32)
        for row, target, first, near in (
            (anchor - 1, 0, 0, 1), (anchor + band, W - 1, r + 2, r + 2),
        ):
            owner = lax.div(row, R)

            def fill(owner=owner, first=first, near=near):
                for f in range(2):
                    value = scale * sum(slots[k][owner, f] for k in ks)
                    fine = jnp.dot(
                        value, wider, precision=lax.Precision.HIGHEST,
                        preferred_element_type=jnp.float32,
                    )
                    dst[f, first, :, 0:c] = fine
                    dst[f, first + 1, :, 0:c] = fine
                left = scale * sum(corners[k][0, owner] for k in ks)
                if N > 2:
                    right = scale * sum(corners[k][1, owner] for k in ks)
                    left = jnp.where(lane[:8] % 2 == 0, left, right)
                for part in range(K // 8):
                    dst[0, near, 8 * part:8 * part + 8, c:c + T] = roll(left, T - 1 - 2 * part)
            pl.when(w == target)(fill)

    def column_sums(ext, rows, out):
        weights = cb[0, :, 0:ext.shape[3]]

        def body(j, _):
            out[pl.ds(j, 1), :] = jnp.sum(weights * ext[0, j + 1], axis=0, keepdims=True)
            return 0
        lax.fori_loop(0, rows + 2, body, 0, unroll=True)

    def advance(ext, rows, lanes, mine, theirs, lap, f, g, store, parts=1, after=None):
        L = lanes + T
        near = lambda x: roll(x, 1) + roll(x, L - 1)

        def inner(j, _):
            x = ext[0, j + 1]
            lap[j] = ext[0, j + 2] + ext[0, j] + near(x) - 4.0 * x
            return 0
        lax.fori_loop(0, rows + 2, inner, 0, unroll=True)
        diffuse, smooth = f * cb[1, :, 0:lanes], g * cb[2, :, 0:lanes]
        couple, advect = f * cb[3, :, 0:lanes], f * cb[4, :, 0:lanes]

        def body(i, _):
            total = lambda j: mine[pl.ds(j, 1), :] + theirs[pl.ds(j, 1), :]
            p0, p1, p2 = total(i), total(i + 1), total(i + 2)
            wide1 = jnp.broadcast_to(p1, (8, L))
            pl_, pr = roll(wide1, 1)[0:1, :lanes], roll(wide1, L - 1)[0:1, :lanes]
            p0, p1, p2 = p0[:, :lanes], p1[:, :lanes], p2[:, :lanes]
            lap_p = p2 + p0 + pr + pl_ - 4.0 * p1
            drp, dcp = 0.5 * (p2 - p0), 0.5 * (pr - pl_)
            l1 = lap[i + 1]
            m1 = l1[:, :lanes]
            lap2 = lap[i + 2][:, :lanes] + lap[i][:, :lanes] + near(l1)[:, :lanes] - 4.0 * m1
            h = ext[0, i + 2][:, :lanes]
            store(0, i, h + diffuse * m1 - smooth * lap2 + couple * lap_p)
            q = ext[1, i + 2]
            qu, qd, q1 = ext[1, i + 1][:, :lanes], ext[1, i + 3][:, :lanes], q[:, :lanes]
            ql, qr = roll(q, 1)[:, :lanes], roll(q, L - 1)[:, :lanes]
            lap_q = qd + qu + qr + ql - 4.0 * q1
            drift = drp * (0.5 * (qd - qu)) + dcp * (0.5 * (qr - ql))
            store(1, i, q1 + diffuse * lap_q - advect * drift)
            return 0
        size = rows // parts
        for part in range(parts):
            lax.fori_loop(part * size, (part + 1) * size, body, 0, unroll=True)
            if after:
                after(part)

    def pack_nest(ref, start, dst, tile):
        dst[tile] = jnp.zeros((K, T), jnp.float32)

        def body(i, _):
            for f in range(2):
                slot = f * r + i
                x = ends(ref[f, i + start], c)
                dst[tile] = jnp.where(lane // 4 == slot, roll(x, 4 * slot + 2), dst[tile])
            return 0
        lax.fori_loop(0, r, body, 0, unroll=True)

    pack[0] = jnp.zeros((K, T), jnp.float32)

    def pack_parent(i, _):
        for f in range(2):
            slot = f * R + i
            x = ends(p_ref[f, i], C)
            pack[0] = jnp.where(lane // 4 == slot, roll(x, 4 * slot + 2), pack[0])
        return 0
    lax.fori_loop(0, R, pack_parent, 0, unroll=True)
    pack_nest(n_ref, 0, pack, 1)
    for slot, row in ((2 * r, 0), (2 * r + 1, R - 1)):
        x = ends(p_ref[0, row], C)
        pack[1] = jnp.where(lane // 4 == slot, roll(x, 4 * slot + 2), pack[1])
    for j in range(5):
        cb[j] = jnp.broadcast_to(cf_ref[:, j:j + 1], cb.shape[1:])
    for f in range(2):
        pe[f, 2:R + 2, :, 0:C] = p_ref[f]
        ne[f, 2:r + 2, :, 0:c] = n_ref[f]
    for cond, first in ((w == 0, 0), (w == W - 1, R + 2)):
        def clear(first=first):
            pe[:, first:first + 2] = jnp.zeros((2, 2, K, C + T), jnp.float32)
        pl.when(cond)(clear)
    pl.semaphore_wait(barrier, count + 1)
    wait_rows = [send_rows(p_ref, 0, pe, R, C), send_rows(n_ref, 0, ne, r, c)]
    wait_packs = send_packs(pack, cr, 1)
    wait_old = send_picks(p_ref, 0)

    left_part = lane % 4 < 2
    side = lambda slot: lax.rem(2 * T - 2 - 4 * slot, T)
    wait_packs()
    m0 = merged(cr, 1, 0, left_part)
    m1 = merged(cr, 1, 1, left_part)

    def unpack_parent(i, _):
        for f in range(2):
            pe[f, i + 2, :, C:C + T] = roll(m0, side(f * R + i))
        return 0
    lax.fori_loop(0, R, unpack_parent, 0, unroll=True)

    def unpack_nest(dst, m):
        def body(i, _):
            for f in range(2):
                dst[f, i + 2, :, c:c + T] = roll(m, side(f * r + i))
            return 0
        lax.fori_loop(0, r, body, 0, unroll=True)
    unpack_nest(ne, m1)

    @pl.when(above)
    def _():
        m = merged(cr, 0, 1, left_part)
        pe[0, 1, :, C:C + T] = roll(m, side(2 * r + 1))
        ne[0, 1, :, c:c + T] = roll(m, side(r - 1))

    @pl.when(below)
    def _():
        m = merged(cr, 2, 1, left_part)
        pe[0, R + 2, :, C:C + T] = roll(m, side(2 * r))
        ne[0, r + 2, :, c:c + T] = roll(m, side(0))

    def share(mine, theirs):
        s = take()
        send(mine, theirs, s, other)
        return lambda: receive(theirs, s)

    wait_rows[0]()
    column_sums(pe, R, psp)
    wait_p = share(psp, prp)
    wait_rows[1]()
    wait_old()
    set_edges(ne, (0,))
    column_sums(ne, r, psn)
    wait_n = share(psn, prn)
    wait_p()

    def store_parent(f, i, v):
        po_ref[f, i] = v

    def store_mid(f, i, v):
        ne2[f, i + 2, :, 0:c] = v

    def store_nest(f, i, v):
        no_ref[f, i] = v

    advance(pe, R, C, psp, prp, lp, 1.0, 1.0, store_parent)
    wait_new = send_picks(po_ref, 1)
    wait_n()
    advance(ne, r, c, psn, prn, ln, 2.0, 8.0, store_mid)
    wait_mid = send_rows(ne2, 2, ne2, r, c)
    pack_nest(ne2, 2, pack2, 0)
    wait_packs2 = send_packs(pack2, cr2, 0)
    wait_new()
    set_edges(ne2, (0, 1))
    wait_packs2()
    unpack_nest(ne2, merged(cr2, 1, 0, left_part))

    @pl.when(above)
    def _():
        ne2[0, 1, :, c:c + T] = roll(merged(cr2, 0, 0, left_part), side(r - 1))

    @pl.when(below)
    def _():
        ne2[0, r + 2, :, c:c + T] = roll(merged(cr2, 2, 0, left_part), side(0))

    wait_mid()
    column_sums(ne2, r, psm)
    wait_m = share(psm, prm)
    wait_m()
    narrower = jnp.where(
        lax.broadcasted_iota(jnp.int32, (c, C), 0) // 2
        == lax.broadcasted_iota(jnp.int32, (c, C), 1), 0.25, 0.0
    )
    base = w * half
    pieces = 2 if half % 2 == 0 else 1
    many = half // pieces
    s_down, s_up = take(pieces * W), take(pieces * W)
    block = lambda at, piece: cg.at[pl.ds(at * half + piece * many, many)]

    def send_coarse(piece):
        for i in range(piece * many, (piece + 1) * many):
            for f in range(2):
                cg[base + i, f] = jnp.dot(
                    no_ref[f, 2 * i] + no_ref[f, 2 * i + 1], narrower,
                    precision=lax.Precision.HIGHEST, preferred_element_type=jnp.float32,
                )
        own = block(w, piece)
        for far in (2, 1):
            send(own, own, s_down + piece * W + w, {"wide": w + far}, w + far < W)
            send(own, own, s_up + piece * W + w, {"wide": w - far}, w - far >= 0)

    advance(ne2, r, c, psm, prm, ln, 2.0, 8.0, store_nest, pieces, send_coarse)
    for hop in (2, 1) + tuple(range(3, W)):
        for piece in range(pieces):
            for first, src, there, to, more in (
                (s_down, jnp.maximum(w - hop, 0), w >= hop, down, below),
                (s_up, jnp.minimum(w + hop, W - 1), w + hop < W, up, above),
            ):
                one, sem = block(src, piece), first + piece * W + src
                receive(one, sem, there)
                if 2 <= hop < W - 1:
                    send(one, one, sem, to, there & more)

    def absorb(i, _):
        at = w * R + i - anchor
        inside = (at >= 0) & (at < band)
        piece = jnp.clip(at, 0, band - 1)
        for f in range(2):
            po_ref[f, i] = jnp.where(inside, cg[piece, f], po_ref[f, i])
        return 0
    lax.fori_loop(0, R, absorb, 0, unroll=True)
    for copy, cond in pending:
        guarded(cond, lambda copy=copy: copy.wait_send())


def shards(
    W, N, parent_state, nest_state, level_weights, diffusion, smoothing, coupling, transport, nest_anchor
):
    p = jnp.swapaxes(parent_state, 1, 2)
    q = jnp.swapaxes(nest_state, 1, 2)
    cf = jnp.stack([level_weights, diffusion, smoothing, coupling, transport], axis=1)
    _, R, K, C = p.shape
    r, c = q.shape[1], q.shape[3]
    D = 1 if N == 2 else 2
    F = lambda *dims: pltpu.VMEM(dims, jnp.float32)
    up8 = lambda x: -(-x // 8) * 8
    sums = lambda rows, lanes: F(up8(rows + 2), lanes + T)
    nsem = 64 + 24 * D + 4 * W * (3 + D)
    vm = pl.BlockSpec(memory_space=pltpu.VMEM)
    a, b = pl.pallas_call(
        functools.partial(kernel, W, N),
        out_shape=(
            jax.ShapeDtypeStruct(p.shape, jnp.float32), jax.ShapeDtypeStruct(q.shape, jnp.float32),
        ),
        in_specs=[pl.BlockSpec(memory_space=pltpu.SMEM), vm, vm, vm],
        out_specs=(vm, vm),
        scratch_shapes=[
            F(2, R + 4, K, C + T), F(2, r + 4, K, c + T), F(2, r + 4, K, c + T),
            F(R + 2, K, C + T), F(r + 2, K, c + T), F(5, K, max(C, c) + T),
            F(2, K, T), F(1, K, T), F(D, 3, 2, K, T), F(D, 3, 1, K, T),
            sums(R, C), sums(R, C), sums(r, c), sums(r, c), sums(r, c), sums(r, c),
            F(2, 2, 2, K, C), F(2, 2, 8, T), F(W, 2, K, C), F(W, 2, K, C), F(D, W, 8, T), F(D, W, 8, T),
            F(W * (r // 2), 2, K, C),
            pltpu.SemaphoreType.DMA((nsem,)), pltpu.SemaphoreType.DMA((nsem,)),
        ],
        compiler_params=pltpu.CompilerParams(
            collective_id=0, has_side_effects=True, vmem_limit_bytes=48 * 1024 * 1024,
        ),
    )(nest_anchor, cf, p, q)
    return jnp.swapaxes(a, 1, 2), jnp.swapaxes(b, 1, 2)


def solution(mesh):
    state = P(None, "lev", ("groups", "wide"), "narrow")
    return jax.shard_map(
        functools.partial(shards, mesh.shape["wide"], mesh.shape["narrow"]),
        mesh=mesh,
        in_specs=(state, state) + (P("lev"),) * 5 + (P("groups"),),
        out_specs=(state, state),
        check_vma=False,
    )
```
